256 devices in a mesh: ens: 16 (over x, y), band: 16 (over z, core).
Axes of the slice: x: 4, y: 4, z: 8, core: 2. Of those that a mesh axis runs over, the one named last changes fastest.
Arguments:
- hidden: float32 [16, 4096, 1024], P('ens', 'band'), may hold values from -6 to 6
- nbr_index: int32 [3, 12288], P(None, 'band'), may hold values from 0 to 4095, as said below
- edge_weight: float32 [3, 12288], P(None, 'band'), may hold values from 0.2 to 1
- band_rows: int32 [16], replicated, may hold values from 1 to 768
- target: float32 [100, 12288], P(None, 'band'), may hold values from -6 to 6
- w_mix: float32 [1024, 1024], replicated, may hold values from -0.1875 to 0.1875
- w_out: float32 [100, 1024], replicated, may hold values from -0.1875 to 0.1875
Outputs:
- grad_hidden: float32 [16, 4096, 1024], P('ens', 'band')
- grad_mix: float32 [1024, 1024], P('band')
- grad_out: float32 [100, 1024], replicated
The draws below stay inside these ranges and needn't reach their ends.
Inputs may be any that keep to these rules, and one draw needn't show every extreme that they name: `nbr_index`: every index of a grid slot in band b lies in b * 256 - 64 to (b + 1) * 256 + 63; both ends are used in every inner band, and live slots of every band but the last read the next band's first rows.
All inputs are finite; a program needn't handle non-finite values.
Results may differ from the reference program's by a relative error of at most 0.023.
Values sent between devices are 32-bit elements; how exact they have to be, the bound alone decides.
No kernel may reach another device: no remote copies, remote signals or barrier semaphores. Data moves between devices by JAX's collectives and lax.ppermute only.
A program may use at most 128 MiB of HBM per device.

```python
import math
import jax
import jax.numpy as jnp
from jax import lax

H = 1024
V = 100
K = 3
G_DEV = 768
NH_DEV = 256
HALO = 64
G_TOTAL = 12288
NH = 4096
MEMBERS = 16
N_BAND = 16


def draw_nbr_index(key, part):
    key = jax.random.fold_in(key, 11)
    slots = jnp.arange(G_DEV * N_BAND, dtype=jnp.int32)
    band_of = slots // G_DEV
    position = slots % G_DEV
    centre = band_of * NH_DEV + position * NH_DEV // G_DEV
    offsets = jax.random.randint(key, (K, G_DEV * N_BAND), -HALO, HALO + 1)
    lowest = jnp.maximum(band_of * NH_DEV - HALO, 0)
    highest = jnp.minimum((band_of + 1) * NH_DEV + HALO - 1, NH_DEV * N_BAND - 1)
    chosen = jnp.clip(centre[None] + offsets, lowest[None], highest[None])
    first_row = jnp.where((position == 0) & (band_of > 0), band_of * NH_DEV - HALO, chosen[0])
    first_row = jnp.where((position == G_DEV - 1) & (band_of < N_BAND - 1), (band_of + 1) * NH_DEV + HALO - 1, first_row)
    early_count = max(G_DEV // 8, 1)
    forward_row = (band_of + 1) * NH_DEV + position % HALO
    second_row = jnp.where((position < early_count) & (band_of < N_BAND - 1), forward_row, chosen[1])
    return jnp.concatenate([first_row[None], second_row[None], chosen[2:]], axis=0).astype(jnp.int32)


def draw_band_rows(key, part):
    key = jax.random.fold_in(key, 23)
    bands = jnp.arange(N_BAND, dtype=jnp.int32)
    distance = jnp.minimum(bands, N_BAND - 1 - bands)
    base = G_DEV // 4 + 3 * G_DEV // 4 * distance * 2 // max(N_BAND - 1, 1)
    jitter = jax.random.randint(key, (N_BAND,), 0, G_DEV // 8 + 1)
    rows = jnp.clip(base - jitter, 1, G_DEV)
    return jnp.where(bands == N_BAND // 2, G_DEV, rows).astype(jnp.int32)


def shard_levels(own_key, extent, cuts, low, high):
    def one(dim, shards_of):
        draws = jax.random.uniform(jax.random.fold_in(jax.random.fold_in(own_key, 6), dim), (shards_of,), jnp.float32, low / len(cuts), high / len(cuts))
        return jnp.repeat(jnp.exp(draws), extent[dim] // shards_of).reshape((-1,) + (1,) * (len(extent) - dim - 1))

    loudness = one(*cuts[0])
    for cut in cuts[1:]:
        loudness = loudness * one(*cut)
    return loudness


def normal_values(key, shape, width, reach, cuts=(), kind=jnp.bfloat16):
    values = width * jax.random.normal(key, shape, jnp.float32)
    if cuts:
        values = values * shard_levels(key, shape, cuts, -0.22, 0.18)
    return jnp.clip(values, -reach, reach).astype(kind)


def setup_inputs(seed: int = 0) -> dict:
    splits = jax.random.split(jax.random.key(seed), 8)
    hidden = normal_values(splits[0], (MEMBERS, NH, H), 1.0, 6.0, ((0, 16), (1, 16)), jnp.float32)
    nbr_index = draw_nbr_index(jax.random.fold_in(splits[7], 71), 0)
    edge_weight = jnp.clip(jnp.exp(math.log(1.0) - 1.609438 * jax.random.uniform(splits[2], (K, G_TOTAL), jnp.float32) ** shard_levels(splits[2], (K, G_TOTAL), ((1, 16),), -0.2, 0.2)), 0.2, 1.0)
    band_rows = draw_band_rows(jax.random.fold_in(splits[7], 71), 0)
    target = normal_values(splits[4], (V, G_TOTAL), 1.0, 6.0, ((1, 16),), jnp.float32)
    w_mix = normal_values(splits[5], (H, H), H ** -0.5, 0.1875, (), jnp.float32)
    w_out = normal_values(splits[6], (V, H), H ** -0.5, 0.1875, (), jnp.float32)
    return dict(hidden=hidden, nbr_index=nbr_index, edge_weight=edge_weight, band_rows=band_rows, target=target, w_mix=w_mix, w_out=w_out)


HIGH = lax.Precision.HIGHEST

def decode(member_hidden, nbr_index, edge_weight, w_mix):
    message = edge_weight[0][:, None] * member_hidden[nbr_index[0]]
    for slot in range(1, K):
        message = message + edge_weight[slot][:, None] * member_hidden[nbr_index[slot]]
    pre_act = jnp.dot(message, w_mix, precision=HIGH)
    activ, gelu_back = jax.vjp(jax.nn.gelu, pre_act)
    return (message, message + activ, gelu_back)

def reference(hidden, nbr_index, edge_weight, band_rows, target, w_mix, w_out):
    slots = jnp.arange(G_TOTAL, dtype=jnp.int32)
    live = (slots % G_DEV < band_rows[slots // G_DEV]).astype(jnp.float32)

    def predict(member_hidden):
        message, node, gelu_back = decode(member_hidden, nbr_index, edge_weight, w_mix)
        return jnp.dot(w_out, node.T, precision=HIGH)
    preds = lax.map(predict, hidden)

    def make_seed(own):
        pairs = lax.optimization_barrier(jnp.sum(jnp.sign(own[None] - preds), axis=0))
        return live[None] * (jnp.sign(own - target) - pairs / (MEMBERS - 1.0))
    seeds = lax.map(make_seed, preds)

    def backward(carry, inputs):
        member_hidden, seed_field = inputs
        message, node, gelu_back = decode(member_hidden, nbr_index, edge_weight, w_mix)
        d_node = jnp.dot(seed_field.T, w_out, precision=HIGH)
        d_pre = gelu_back(d_node)[0]
        d_message = d_node + jnp.dot(d_pre, w_mix.T, precision=HIGH)
        grad_rows = jnp.zeros((NH, H), jnp.float32)
        for slot in range(K):
            grad_rows = grad_rows.at[nbr_index[slot]].add(edge_weight[slot][:, None] * d_message)
        mix_sum = carry[0] + jnp.dot(message.T, d_pre, precision=HIGH)
        out_sum = carry[1] + jnp.dot(seed_field, node, precision=HIGH)
        return ((mix_sum, out_sum), grad_rows)
    start = (jnp.zeros((H, H), jnp.float32), jnp.zeros((V, H), jnp.float32))
    totals, grad_hidden = lax.scan(backward, start, (hidden, seeds))
    live_count = jnp.sum(band_rows).astype(jnp.float32)
    scale = 1.0 / jnp.sqrt(MEMBERS * live_count)
    return (grad_hidden, scale * totals[0], scale * totals[1])
```

```python
import math

import jax
import jax.numpy as jnp
from jax import lax
from jax.experimental import pallas as pl
from jax.experimental.pallas import tpu as pltpu
from jax.sharding import PartitionSpec as P

K = 3
HALO = 64
LANES = 128
TILE = 256
GELU_C = math.sqrt(2.0 / math.pi)
F32 = jnp.float32
BF16 = jnp.bfloat16


def split2(x):
    high = x.astype(BF16)
    return high, (x - high.astype(F32)).astype(BF16)


def split3(x):
    high = x.astype(BF16)
    rest = x - high.astype(F32)
    mid = rest.astype(BF16)
    return high, mid, (rest - mid.astype(F32)).astype(BF16)


def mm(a, b):
    return lax.dot_general(a, b, (((1,), (0,)), ((), ())), preferred_element_type=F32)


def mm_nt(a, b):
    return lax.dot_general(a, b, (((1,), (1,)), ((), ())), preferred_element_type=F32)


def stack3(ref, x):
    n = x.shape[0]
    for i, part in enumerate(split3(x)):
        ref[i * n : (i + 1) * n, :] = part


def mm6(a3_ref, b):
    n = a3_ref.shape[0] // 3
    bh, bm, bl = split3(b)
    p = mm(a3_ref[...], bh)
    q = mm(a3_ref[: 2 * n, :], bm)
    small = p[2 * n :] + q[n:] + mm(a3_ref[:n, :], bl)
    return (small + (p[n : 2 * n] + q[:n])) + p[:n]


def edge_matrix(nbr_ref, weight_ref, rows):
    slots = nbr_ref.shape[1]
    ext = rows + 2 * HALO
    base = lax.axis_index("band") * rows - HALO
    node_id = lax.broadcasted_iota(jnp.int32, (ext, slots), 0)
    total = jnp.zeros((ext, slots), F32)
    for k in range(K):
        local = nbr_ref[k : k + 1, :] - base
        total = total + jnp.where(node_id == local, weight_ref[k : k + 1, :], 0.0)
    return total


def own_kernel(own_ref, own_col, mix_ref, proj_ref, last_ref, first_ref, own3):
    rows = own_ref.shape[0]

    @pl.when(pl.program_id(0) == 0)
    def _():
        stack3(own3, own_ref[...])

    proj = mm6(own3, mix_ref[...])
    proj_ref[...] = proj
    last_ref[0] = own_col[rows - HALO :, :]
    last_ref[1] = proj[rows - HALO :]
    first_ref[0] = own_col[:HALO, :]
    first_ref[1] = proj[:HALO]


def terms6(ref, value, at):
    n = value.shape[0]
    vh, vm, vl = split3(value)
    for i, part in enumerate((vl, vm, vm, vh, vh, vh)):
        ref[i * n : (i + 1) * n, at : at + TILE] = part


def inner_kernel(own_col, proj_ref, nbr_ref, weight_ref, part_ref, rim6_ref, a6, x6):
    rows = own_col.shape[0]

    @pl.when(pl.program_id(0) == 0)
    def _():
        edges = edge_matrix(nbr_ref, weight_ref, rows)
        ah, am, al = split3(edges[HALO : HALO + rows].T)
        for i, part in enumerate((ah, am, ah, al, am, ah)):
            a6[:, i * rows : (i + 1) * rows] = part
        rim = jnp.concatenate([edges[:HALO], edges[HALO + rows :]], axis=0)
        ah, am, al = split3(rim.T)
        for i, part in enumerate((ah, am, ah, al, am, ah)):
            rim6_ref[:, i * 2 * HALO : (i + 1) * 2 * HALO] = part

    terms6(x6, own_col[...], 0)
    terms6(x6, proj_ref[...], TILE)
    both = mm(a6[...], x6[...])
    part_ref[0] = both[:, :TILE]
    part_ref[1] = both[:, TILE:]


def forward_kernel(part_ref, rim6_ref, before_ref, after_ref, out_ref, pred_ref, node_ref, slope_ref, x6, wo):
    outs = out_ref.shape[0]

    @pl.when(pl.program_id(0) == 0)
    def _():
        wo[...] = jnp.zeros_like(wo)
        pred_ref[...] = jnp.zeros_like(pred_ref)

    for half in range(2):
        terms6(x6, jnp.concatenate([before_ref[half], after_ref[half]], axis=0), half * TILE)
    both = mm(rim6_ref[...], x6[...])
    message = part_ref[0] + both[:, :TILE]
    pre = part_ref[1] + both[:, TILE:]
    t = jnp.tanh(GELU_C * (pre + 0.044715 * (pre * pre * pre)))
    cdf = 0.5 * (1.0 + t)
    slope_ref[...] = cdf + (0.5 * GELU_C) * pre * (1.0 - t * t) * (1.0 + (3.0 * 0.044715) * (pre * pre))
    node = message + pre * cdf
    node_ref[...] = node
    wo[:outs, :] = out_ref[...]
    nh, nm, nl = split3(node)
    wh, wm, wl = split3(wo[...])
    main = mm_nt(jnp.concatenate([nh, nm], axis=1), jnp.concatenate([jnp.concatenate([wh, wh], axis=1), jnp.concatenate([wm, wm], axis=1)], axis=0))
    small = mm_nt(jnp.concatenate([nh, nl], axis=1), jnp.concatenate([wl, wh], axis=1))
    pred_ref[...] += (small + main[:, LANES:]) + main[:, :LANES]


def is_first_core():
    return lax.axis_index("band") % 2 == 0


def by_core(x):
    blocks = x.reshape(x.shape[0] // (2 * HALO), 2, HALO, x.shape[1])
    first = is_first_core()
    shape = (x.shape[0] // 2, x.shape[1])
    mine = jnp.where(first, blocks[:, 0], blocks[:, 1]).reshape(shape)
    other = jnp.where(first, blocks[:, 1], blocks[:, 0]).reshape(shape)
    return mine, other


def terms3(ref, value, at):
    n = value.shape[1]
    high, low = split2(value)
    ref[:, at : at + n] = high
    ref[:, at + n : at + 2 * n] = low
    ref[:, at + 2 * n : at + 3 * n] = high


def prepare_kernel(before_ref, own_ref, after_ref, nbr_ref, weight_ref, at_ref, mine_ref, other_ref):
    ext = own_ref.shape[0] + 2 * HALO
    at_ref[:ext, :], at_ref[ext:, :] = split2(edge_matrix(nbr_ref, weight_ref, own_ref.shape[0]))
    mine, other = by_core(jnp.concatenate([before_ref[0], own_ref[...], after_ref[0]], axis=0).T)
    terms3(mine_ref, mine, 0)
    other_ref[...] = other


def rank_kernel(all_ref, pairs_ref):
    members = all_ref.shape[0]
    rows = all_ref.shape[1]

    def step(r, carry):
        at = pl.ds(pl.multiple_of(r * 8, 8), 8)
        values = [all_ref[e, at, :] for e in range(members)]
        sums = [jnp.zeros_like(values[0]) for _ in range(members)]
        for e in range(members):
            for f in range(e + 1, members):
                sign = jnp.where(values[e] > values[f], 1.0, 0.0) - jnp.where(values[e] < values[f], 1.0, 0.0)
                sums[e] = sums[e] + sign
                sums[f] = sums[f] - sign
        for e in range(members):
            pairs_ref[e, at, :] = sums[e]
        return carry

    lax.fori_loop(0, rows // 8, step, 0)


def backward_kernel(members, pred_ref, pairs_ref, target_ref, live_ref, at_ref, node_ref, slope_ref, out_ref,
                    g_ref, out_grad_ref, q_ref, seed_s, seed_t, wo, tgt):
    ext = at_ref.shape[0] // 2
    outs = out_ref.shape[0]
    unit = 1.0 / (members - 1.0)

    @pl.when(pl.program_id(0) == 0)
    def _():
        wo[...] = jnp.zeros_like(wo)
        tgt[...] = jnp.zeros_like(tgt)
        tgt[:outs, :] = target_ref[...]
        target = tgt[...].T
        pred = pred_ref[...]
        sign = jnp.where(pred > target, 1.0, 0.0) - jnp.where(pred < target, 1.0, 0.0)
        live = lax.broadcasted_iota(jnp.int32, pred.shape, 0) < live_ref[lax.axis_index("band")]
        seed = jnp.where(live, (members - 1.0) * sign - pairs_ref[...], 0.0)
        seed_b = seed.astype(BF16)
        seed_s[:, :LANES] = seed_b
        seed_s[:, LANES:] = seed_b
        seed_t[...] = seed.T.astype(BF16)
        q = mm(at_ref[...], seed_b)
        q_ref[...] = (q[:ext] + q[ext:]) * unit

    wo[:outs, :] = out_ref[...]
    wh, wl = split2(wo[...])
    d_node = mm(seed_s[...], jnp.concatenate([wh, wl], axis=0))
    d_pre = d_node * unit * slope_ref[...]
    dh, dl = split2(d_pre)
    p = mm(at_ref[...], dh)
    g_ref[:ext, :] = p[:ext] + (p[ext:] + mm(at_ref[:ext, :], dl))
    nh, nl = split2(node_ref[...])
    mine, other = by_core((mm(seed_t[...], nh) + mm(seed_t[...], nl)) * unit)
    out_grad_ref[...] = mine
    g_ref[ext:, :] = other


def mix_kernel(members, live_ref, mine_ref, facing_ref, g_ref, got_ref, out_grad_ref, piece_ref, e6):
    ext = facing_ref.shape[1]
    half = mine_ref.shape[0]

    @pl.when(pl.program_id(0) == 0)
    def _():
        e6[:, : 3 * ext] = mine_ref[...]
        terms3(e6, facing_ref[...], 3 * ext)

    count = live_ref[0]
    for i in range(1, live_ref.shape[0]):
        count = count + live_ref[i]
    scale = 1.0 / jnp.sqrt(jnp.full((1, TILE), members, F32) * count.astype(F32))
    gh, gl = split2(g_ref[:ext, :] * scale)
    fh, fl = split2(got_ref[:ext, :] * scale)

    def store(z, block):
        for r in range(4):
            piece_ref[r, 0, z] = block[16 * r : 16 * r + 16]

    store(half // HALO, (out_grad_ref[...] + got_ref[ext:, :]) * scale)
    d6 = jnp.concatenate([gh, gh, gl, fh, fh, fl], axis=0)
    for i in range(half // TILE):
        tile = mm(e6[TILE * i : TILE * (i + 1), :], d6)
        for z in range(TILE // HALO):
            store((TILE // HALO) * i + z, tile[HALO * z : HALO * (z + 1)])


def hidden_kernel(g_ref, q_ref, mix_ref, out_ref, upper_ref, middle_ref, lower_ref, g2, wo):
    rows = middle_ref.shape[0]
    outs = out_ref.shape[0]
    ext = q_ref.shape[0]

    @pl.when(pl.program_id(0) == 0)
    def _():
        g2[:ext, :], g2[ext:, :] = split2(g_ref[:ext, :])
        wo[...] = jnp.zeros_like(wo)

    wo[:outs, :] = out_ref[...]
    qh, ql = split2(q_ref[...])
    wh, wl = split2(wo[...])
    mh, ml = split2(mix_ref[...])
    p = mm_nt(g2[...], mh)
    total = p[:ext] + (p[ext:] + mm_nt(g2[:ext, :], ml))
    total = total + (mm(qh, wl) + mm(ql, wh) + mm(qh, wh))
    upper_ref[...] = total[:HALO]
    middle_ref[...] = total[HALO : HALO + rows]
    lower_ref[...] = total[HALO + rows :]


def whole(shape):
    return pl.BlockSpec(shape, lambda j: (0,) * len(shape))


def columns(rows):
    return pl.BlockSpec((rows, TILE), lambda j: (0, j))


def call(kernel, steps, ins, outs, scratch, args, flops, limit=60):
    return pl.pallas_call(
        kernel,
        grid=(steps,),
        out_shape=[jax.ShapeDtypeStruct(s, d) for s, d, _ in outs],
        in_specs=ins,
        out_specs=[spec for _, _, spec in outs],
        scratch_shapes=[pltpu.VMEM(s, d) for s, d in scratch],
        compiler_params=pltpu.CompilerParams(vmem_limit_bytes=limit * 1024 * 1024),
        cost_estimate=pl.CostEstimate(flops=flops, bytes_accessed=6_000_000, transcendentals=0),
    )(*args)


def body(hidden, nbr_index, edge_weight, band_rows, target, w_mix, w_out):
    own = hidden[0]
    rows, width = own.shape
    slots = target.shape[1]
    outs = w_out.shape[0]
    bands = lax.axis_size("band")
    members = lax.axis_size("ens")
    ext = rows + 2 * HALO
    tiles = width // TILE
    up = [(i, i + 1) for i in range(bands - 1)]
    down = [(j, i) for i, j in up]
    pair = [(i, i ^ 1) for i in range(bands)]

    rim = pl.BlockSpec((2, HALO, TILE), lambda j: (0, 0, j))
    proj, last, first = call(
        own_kernel, tiles,
        [whole((rows, width)), columns(rows), columns(width)],
        [((rows, width), F32, columns(rows)), ((2, HALO, width), F32, rim), ((2, HALO, width), F32, rim)],
        [((3 * rows, width), BF16)],
        (own, own, w_mix),
        12 * rows * width * width,
    )
    before = lax.ppermute(last, "band", up)
    after = lax.ppermute(first, "band", down)
    edges = [whole((K, slots))] * 2
    both = pl.BlockSpec((2, slots, TILE), lambda j: (0, 0, j))
    part, rim6 = call(
        inner_kernel, tiles,
        [columns(rows), columns(rows)] + edges,
        [((2, slots, width), F32, both), ((slots, 12 * HALO), BF16, whole((slots, 12 * HALO)))],
        [((slots, 6 * rows), BF16), ((6 * rows, 2 * TILE), BF16)],
        (own, proj, nbr_index, edge_weight),
        24 * slots * rows * width,
    )
    pred, node, slope = call(
        forward_kernel, tiles,
        [both, whole((slots, 12 * HALO)), rim, rim, columns(outs)],
        [((slots, LANES), F32, whole((slots, LANES))), ((slots, width), F32, columns(slots)), ((slots, width), F32, columns(slots))],
        [((12 * HALO, 2 * TILE), BF16), ((LANES, TILE), F32)],
        (part, rim6, before, after, w_out),
        24 * slots * ext * width,
    )
    share = slots // members
    half = width // 2
    everyone = lax.all_to_all(pred.reshape(members, share, LANES), "ens", 0, 0, tiled=True)
    at2, mine, other = call(
        prepare_kernel, 1,
        [whole((2, HALO, width)), whole((rows, width)), whole((2, HALO, width))] + edges,
        [((2 * ext, slots), BF16, whole((2 * ext, slots))), ((half, 3 * ext), BF16, whole((half, 3 * ext))), ((half, ext), F32, whole((half, ext)))],
        [],
        (before, own, after, nbr_index, edge_weight),
        4_000_000_000,
    )
    (pairs,) = call(
        rank_kernel, 1, [whole((members, share, LANES))], [((members, share, LANES), F32, whole((members, share, LANES)))], [], (everyone,), 10_000_000, 8
    )
    pairs = lax.all_to_all(pairs, "ens", 0, 0, tiled=True).reshape(slots, LANES)

    facing = lax.ppermute(other, "band", pair)
    g, out_grad, q = call(
        lambda *refs: backward_kernel(members, *refs), tiles,
        [whole((slots, LANES))] * 2 + [whole((outs, slots)), pl.BlockSpec(memory_space=pltpu.SMEM), whole((2 * ext, slots))]
        + [columns(slots)] * 2 + [columns(outs)],
        [((ext + HALO, width), F32, columns(ext + HALO)), ((HALO, width), F32, columns(HALO)), ((ext, LANES), F32, whole((ext, LANES)))],
        [((slots, 2 * LANES), BF16), ((LANES, slots), BF16), ((LANES, TILE), F32), ((LANES, slots), F32)],
        (pred, pairs, target, band_rows, at2, node, slope, w_out),
        6 * ext * width * width,
    )
    got = lax.ppermute(g, "band", pair)
    lines = bands // 2 + 1
    piece = (members // tiles, tiles, lines, 16, TILE)
    (part,) = call(
        lambda *refs: mix_kernel(members, *refs), tiles,
        [pl.BlockSpec(memory_space=pltpu.SMEM), whole((half, 3 * ext)), whole((half, ext)), columns(ext + HALO), columns(ext + HALO), columns(HALO)],
        [(piece, F32, pl.BlockSpec((members // tiles, 1, lines, 16, TILE), lambda j: (0, j, 0, 0, 0)))],
        [((half, 6 * ext), BF16)],
        (band_rows, mine, facing, g, got, out_grad),
        6 * ext * width * width,
    )
    part, g = lax.optimization_barrier((part, g))
    upper, middle, lower = call(
        hidden_kernel, tiles,
        [whole((ext + HALO, width)), whole((ext, LANES)), pl.BlockSpec((TILE, width), lambda j: (j, 0)), columns(outs)],
        [((HALO, width), F32, columns(HALO)), ((rows, width), F32, columns(rows)), ((HALO, width), F32, columns(HALO))],
        [((2 * ext, width), BF16), ((LANES, TILE), F32)],
        (g, q, w_mix, w_out),
        6 * ext * width * width,
    )
    from_next = lax.ppermute(upper, "band", down)
    from_previous = lax.ppermute(lower, "band", up)
    grad_hidden = jnp.concatenate(
        [middle[:HALO] + from_previous, middle[HALO : rows - HALO], middle[rows - HALO :] + from_next], axis=0
    )

    position = lax.axis_index("band")
    core, chip = position % 2, position // 2
    part = part.reshape(members, lines, 16, TILE)
    part = lax.all_to_all(part, "ens", 0, 0, tiled=True)
    part, grad_hidden = lax.optimization_barrier((part, grad_hidden))
    part = jnp.sum(part, axis=0)
    mix_part, out_part = part[:-1], part[-1:]
    step = 1
    while step < bands // 2:
        split = mix_part.reshape((-1, 2) + mix_part.shape[1:])
        high = (chip // step) % 2 == 1
        away = jnp.where(high, split[:, 0], split[:, 1])
        here = jnp.where(high, split[:, 1], split[:, 0])
        moved = lax.ppermute(jnp.concatenate([away, out_part], axis=0), "band", [(i, i ^ (2 * step)) for i in range(bands)])
        mix_part = here + moved[:-1]
        out_part = out_part + moved[-1:]
        step *= 2
    part = jnp.concatenate([mix_part, out_part], axis=0)
    total = lax.all_to_all(jnp.broadcast_to(part[None], (members, 2, 16, TILE)), "ens", 0, 0, tiled=True)
    total = total.reshape(members // tiles, tiles, 2, 16, TILE).transpose(2, 0, 3, 1, 4).reshape(2, HALO, width)
    halves = jnp.stack([total[1], lax.ppermute(total[1], "band", pair)])
    grad_out = jnp.where(core == 0, halves, halves[::-1]).reshape(2 * HALO, width)[:outs]
    return (grad_hidden[None], total[0], grad_out)


def solution(mesh):
    placed = (
        P("ens", "band", None),
        P(None, "band"),
        P(None, "band"),
        P(),
        P(None, "band"),
        P(),
        P(),
    )
    return jax.shard_map(
        body,
        mesh=mesh,
        in_specs=placed,
        out_specs=(P("ens", "band", None), P("band", None), P()),
        check_vma=False,
    )
```
